32 devices in a mesh: groups: 2 (over x), pair: 16 (over z, y, core).
Axes of the slice: x: 2, y: 2, z: 4, core: 2. Of those that a mesh axis runs over, the one named last changes fastest.
Arguments:
- amplitudes: bfloat16 [4096, 3600], P(('groups', 'pair')), parts along dimension 0, may hold values from -6 to 6
- pno_coef: bfloat16 [4096, 60, 256], P(('groups', 'pair')), parts along dimension 0, may hold values from -0.375 to 0.375
- metric: bfloat16 [512, 256], P('groups'), parts along dimension 0
- energies: float32 [4096, 60], P(('groups', 'pair')), parts along dimension 0, may hold values from 0.1 to 1
- pno_count: int32 [4096], P(('groups', 'pair')), parts along dimension 0, may hold values from 15 to 60, as said below
- cpl_self: int32 [8192], P(('groups', 'pair')), parts along dimension 0, may hold values from 0 to 127
- cpl_slot: int32 [8192], P(('groups', 'pair')), parts along dimension 0, may hold values from 0 to 63, as said below
- partner_list: int32 [2048], P(('groups', 'pair')), parts along dimension 0, may hold values from 0 to 2047, as said below
Outputs:
- residual: bfloat16 [4096, 3600], P(('groups', 'pair')), parts along dimension 0
The draws below stay inside these ranges and needn't reach their ends.
There are 2 independent parts, one for each index of `groups`. The reference program is written for one: setup_inputs(seed, part) draws one part's arguments, and reference() takes and returns one part's arrays. A program takes and returns all parts, laid end to end along the dimension named above; each array names one. Nothing has to cross between parts.
Inputs may be any that keep to these rules, and one draw needn't show every extreme that they name: `pno_count`: every fragment has a pair with 60 natural orbitals. `cpl_slot`: every entry of a device's partner list is named by at least one of that device's couplings. `partner_list`: in each device's block of 64 entries, entry j * 4 + k names a pair owned by device j (its index // 128 is j), and the block's entries are distinct.
All inputs are finite; a program needn't handle non-finite values.
Results may differ from the reference program's by a relative error of at most 0.0065.
Values may be sent and summed in bfloat16 or wider, within the bound.
A program may use at most 128 MiB of HBM per device.

```python
import math
import jax
import jax.numpy as jnp
from jax import lax

NPNO = 60
DOM = 256
PAIR_DEV = 128
CPL_DEV = 256
CAP = 4
PAIRS = 2048
CPLS = 4096
N_PAIR = 16


def draw_metric(key, part):
    key = jax.random.fold_in(key, 11)
    first, second = jax.random.split(key)
    spread = jax.random.normal(first, (DOM, DOM), jnp.float32)
    spread = (spread + spread.T) * (0.45 / math.sqrt(DOM))
    diagonal = jax.random.uniform(second, (DOM,), jnp.float32, 0.7, 1.3)
    return (spread + jnp.eye(DOM, dtype=jnp.float32) * diagonal[None, :]).astype(jnp.bfloat16)


def draw_pno_count(key, part):
    key = jax.random.fold_in(key, 5)
    first, second = jax.random.split(key)
    counts = jax.random.randint(first, (PAIRS,), NPNO // 4, NPNO + 1)
    chosen = jax.random.randint(second, (), 0, PAIRS)
    return jnp.where(jnp.arange(PAIRS) == chosen, NPNO, counts).astype(jnp.int32)


def draw_cpl_slot(key, part):
    key = jax.random.fold_in(key, 9)
    entries = N_PAIR * CAP

    def one_device(device_key):
        k_cover, k_extra, k_order = jax.random.split(device_key, 3)
        cover = jax.random.permutation(k_cover, entries)
        extra = jax.random.randint(k_extra, (CPL_DEV - entries,), 0, entries)
        every = jnp.concatenate([cover, extra])
        return every[jax.random.permutation(k_order, CPL_DEV)]
    device_keys = jax.random.split(key, N_PAIR)
    return jax.vmap(one_device)(device_keys).reshape(-1).astype(jnp.int32)


def draw_partner_list(key, part):
    key = jax.random.fold_in(key, 7)

    def one_owner(owner_key):
        return jax.random.permutation(owner_key, PAIR_DEV)[:CAP]
    owner_keys = jax.random.split(key, N_PAIR * N_PAIR)
    local = jax.vmap(one_owner)(owner_keys).reshape(N_PAIR, N_PAIR, CAP)
    owners = jnp.arange(N_PAIR, dtype=jnp.int32)[None, :, None]
    return (owners * PAIR_DEV + local).reshape(-1).astype(jnp.int32)


def place_ends(values, key, smallest, largest):
    longest = values.shape.index(max(values.shape))
    spots = []
    for shift in (0, 1):
        where = [jax.random.randint(jax.random.fold_in(key, axis), (), 0, length) for axis, length in enumerate(values.shape)]
        where[longest] = (where[longest] + shift) % values.shape[longest]
        spots.append(tuple(where))
    return values.at[spots[0]].set(smallest).at[spots[1]].set(largest)


def steps_of(own_key, extent, pieces, low, top_value):
    level = 1.0
    for dim, shards_of in pieces:
        steps = jax.random.uniform(jax.random.fold_in(jax.random.fold_in(own_key, 6), dim), (shards_of,), jnp.float32, low / len(pieces), top_value / len(pieces))
        level = level * jnp.repeat(jnp.exp(steps), extent[dim] // shards_of).reshape((-1,) + (1,) * (len(extent) - 1 - dim))
    return level


def gaussian(rng, extent, scale, most, cuts=(), kind=jnp.bfloat16):
    drawn = jax.random.normal(rng, extent, jnp.float32) * scale
    if len(cuts) > 0:
        drawn = steps_of(rng, extent, cuts, -0.22, 0.18) * drawn
    return jnp.clip(drawn, min=-most, max=most).astype(kind)


def setup_inputs(seed: int = 0, part: int = 0) -> dict:
    seeds = jax.random.split(jax.random.key(seed), 9)
    part_splits = jax.random.split(jax.random.fold_in(seeds[8], part), 9)
    return {
        "amplitudes": gaussian(part_splits[0], (PAIRS, NPNO * NPNO), 1.0, 6.0, ((0, 16),)),
        "pno_coef": gaussian(part_splits[1], (PAIRS, NPNO, DOM), DOM ** -0.5, 0.375, ((0, 16),)),
        "metric": draw_metric(jax.random.fold_in(jax.random.fold_in(seeds[8], part), 71), part),
        "energies": jnp.clip(jnp.exp(math.log(1.0) - 2.3025851 * jax.random.uniform(part_splits[3], (PAIRS, NPNO), jnp.float32) ** steps_of(part_splits[3], (PAIRS, NPNO), ((0, 16),), -0.2, 0.2)), 0.1, 1.0),
        "pno_count": draw_pno_count(jax.random.fold_in(jax.random.fold_in(seeds[8], part), 71), part),
        "cpl_self": place_ends(jax.random.randint(part_splits[5], (CPLS,), 0, PAIR_DEV), jax.random.fold_in(part_splits[5], 1), 0, PAIR_DEV - 1).astype(jnp.int32),
        "cpl_slot": draw_cpl_slot(jax.random.fold_in(jax.random.fold_in(seeds[8], part), 71), part),
        "partner_list": draw_partner_list(jax.random.fold_in(jax.random.fold_in(seeds[8], part), 71), part),
    }


def couple(w_self, t_self, q_other, t_other):
    count = w_self.shape[0]
    intersection = jnp.einsum('crk,csk->rsc', w_self.astype(jnp.float32), q_other.astype(jnp.float32)).astype(jnp.bfloat16)
    over_f = intersection.astype(jnp.float32)
    other_t = t_other.T.reshape(NPNO, NPNO, count).astype(jnp.float32)
    self_t = t_self.T.reshape(NPNO, NPNO, count).astype(jnp.float32)
    left_side = jnp.einsum('rsc,stc->rtc', over_f, other_t).astype(jnp.bfloat16)
    to_self = jnp.einsum('rtc,utc->ruc', left_side.astype(jnp.float32), over_f).astype(jnp.bfloat16)
    projected = jnp.einsum('rsc,rtc->stc', over_f, self_t).astype(jnp.bfloat16)
    to_other = jnp.einsum('stc,tuc->suc', projected.astype(jnp.float32), over_f).astype(jnp.bfloat16)
    return to_self.reshape(NPNO * NPNO, count).T, to_other.reshape(NPNO * NPNO, count).T


def reference(amplitudes, pno_coef, metric, energies, pno_count, cpl_self, cpl_slot, partner_list):
    live_rows = jnp.arange(NPNO, dtype=jnp.int32)[None, :] < pno_count[:, None]
    tile_live = jnp.repeat(live_rows, NPNO, axis=1) & jnp.tile(live_rows, (1, NPNO))
    tiles = jnp.where(tile_live, amplitudes, jnp.zeros_like(amplitudes))
    vectors = jnp.where(live_rows[:, :, None], pno_coef, jnp.zeros_like(pno_coef))
    weighted = jnp.dot(vectors.reshape(-1, DOM), metric, preferred_element_type=jnp.float32)
    weighted = weighted.astype(jnp.bfloat16).reshape(PAIRS, NPNO, DOM)
    own_pair = (jnp.arange(N_PAIR, dtype=jnp.int32)[:, None] * PAIR_DEV + cpl_self.reshape(N_PAIR, CPL_DEV)).astype(jnp.int32)
    slot_rows = cpl_slot.reshape(N_PAIR, CPL_DEV).astype(jnp.int32)
    listed_rows = partner_list.reshape(N_PAIR, N_PAIR * CAP).astype(jnp.int32)

    def one_block(summed, blocks):
        mine, slot, listed = blocks
        other = listed[slot]
        to_self, to_other = couple(weighted[mine], tiles[mine], vectors[other], tiles[other])
        summed = summed.at[mine].add(to_self.astype(jnp.float32))
        slot_sum = jnp.zeros((N_PAIR * CAP, NPNO * NPNO), jnp.float32).at[slot].add(to_other.astype(jnp.float32))
        back = lax.optimization_barrier(slot_sum.astype(jnp.bfloat16)).astype(jnp.float32)
        summed = summed.at[listed].add(back)
        return summed, None

    start = jnp.zeros((PAIRS, NPNO * NPNO), jnp.float32)
    summed, unused = lax.scan(one_block, start, (own_pair, slot_rows, listed_rows))
    energy_sum = jnp.repeat(energies, NPNO, axis=1) + jnp.tile(energies, (1, NPNO))
    result = energy_sum * tiles.astype(jnp.float32) - summed
    return jnp.where(tile_live, result, jnp.zeros_like(result)).astype(jnp.bfloat16)
```

```python
import functools

import jax
import jax.numpy as jnp
from jax import lax
from jax.experimental import pallas as pl
from jax.experimental.pallas import tpu as pltpu
from jax.sharding import PartitionSpec as P

F32 = jnp.float32
BF16 = jnp.bfloat16
VMEM = pl.BlockSpec(memory_space=pltpu.VMEM)
SMEM = pl.BlockSpec(memory_space=pltpu.SMEM)
LIMIT = 60 * 1024 * 1024
WIDE = 64
LANES = 128
NT = (((1,), (1,)), ((), ()))


def halves(x):
    lane = lax.broadcasted_iota(jnp.int32, x.shape, 1)
    return jnp.where(lane < WIDE, x, 0.0), jnp.where(lane < WIDE, 0.0, x)


def kernel(
    peers, cap, width, group,
    count_s, self_s, slot_s, count_ref, self_ref, slot_ref, req_ref, en_ref, metric_ref, amp_ref, pno_ref,
    out_ref,
    asked_v, asked_s, amp32, vlo, vhi, tscr, v_ref, w_ref, t_ref, sendv, sendt, gotv, gott, ot_ref,
    sendr, gotr, ret32, own32, back32, hote, hoto, en64,
    local_sem, req_send, req_recv, vec_send, vec_recv, tile_send, tile_recv, back_send, back_recv,
):
    me = lax.axis_index("pair")
    pairs = count_ref.shape[1]
    domain = metric_ref.shape[0]
    couplings = self_ref.shape[1]
    slots = peers * cap
    batches = couplings // 2
    blocks = gott.shape[2] // LANES

    def peer(d):
        return lax.rem(me + d, peers)

    def remote(src, dst, send, recv, d):
        return pltpu.make_async_remote_copy(
            src_ref=src, dst_ref=dst, send_sem=send.at[d], recv_sem=recv.at[d],
            device_id={"pair": peer(d)}, device_id_type=pl.DeviceIdType.MESH,
        )

    def req_copy(d):
        return remote(req_ref.at[peer(d)], asked_v.at[me], req_send, req_recv, d)

    def vec_copy(d):
        return remote(
            sendv.at[pl.ds(peer(d) * cap, cap)], gotv.at[pl.ds(me * cap, cap)], vec_send, vec_recv, d
        )

    def tile_copy(d):
        return remote(sendt.at[peer(d)], gott.at[me], tile_send, tile_recv, d)

    def back_copy(d):
        return remote(sendr.at[peer(d)], gotr.at[me], back_send, back_recv, d)

    barrier = pltpu.get_barrier_semaphore()

    @pl.loop(1, peers)
    def _(d):
        pl.semaphore_signal(
            barrier, inc=1, device_id={"pair": peer(d)}, device_id_type=pl.DeviceIdType.MESH
        )

    pl.semaphore_wait(barrier, peers - 1)

    @pl.loop(1, peers)
    def _(d):
        req_copy(d).start()

    own_req = pltpu.make_async_copy(req_ref.at[me], asked_v.at[me], local_sem.at[0])
    own_req.start()

    for r in range(width):
        x = pno_ref[r].astype(F32)
        vlo[pl.ds(r * pairs, pairs), :] = x[:, :LANES]
        vhi[pl.ds(r * pairs, pairs), :] = x[:, LANES:]
    for r in range(width, WIDE):
        vlo[pl.ds(r * pairs, pairs), :] = jnp.zeros((pairs, LANES), F32)
        vhi[pl.ds(r * pairs, pairs), :] = jnp.zeros((pairs, LANES), F32)
    row = lax.broadcasted_iota(jnp.int32, (WIDE, LANES), 0)

    @pl.loop(0, pairs // 4)
    def _(g):
        for k in range(4):
            p = g * 4 + k
            live = row < count_s[p]
            lo = jnp.where(live, vlo[pl.ds(p, WIDE, stride=pairs), :], 0.0)
            hi = jnp.where(live, vhi[pl.ds(p, WIDE, stride=pairs), :], 0.0)
            v_ref[p, :, pl.ds(0, LANES)] = lo.astype(BF16)
            v_ref[p, :, pl.ds(LANES, LANES)] = hi.astype(BF16)

    rows = amp_ref.shape[0]
    amp32[pl.ds(0, rows), :] = amp_ref[...].astype(F32)
    amp32[pl.ds(rows, amp32.shape[0] - rows), :] = jnp.zeros((amp32.shape[0] - rows, pairs), F32)
    for r in range(WIDE):
        if r < width:
            x = amp32[pl.ds(r * width, WIDE), :]
            x = jnp.concatenate([x, x], axis=0).T
        else:
            x = jnp.zeros((pairs, LANES), F32)
        tscr[pl.ds(r * pairs, pairs), :] = x

    @pl.loop(0, pairs // 4)
    def _(g):
        for k in range(4):
            p = g * 4 + k
            left, right = halves(tscr[pl.ds(p, WIDE, stride=pairs), :])
            t_ref[2 * p] = left.astype(BF16)
            t_ref[2 * p + 1] = right.astype(BF16)

    @pl.loop(1, peers)
    def _(d):
        req_copy(d).wait()

    own_req.wait()
    to_scalar = pltpu.make_async_copy(asked_v, asked_s, local_sem.at[1])
    to_scalar.start()
    to_scalar.wait()

    def gather(to):
        for k in range(cap):
            sendv[to * cap + k] = v_ref[asked_s[to, k, 0]]
        for m in range(blocks):
            x = t_ref[2 * asked_s[to, 2 * m, 0]]
            if 2 * m + 1 < cap:
                x = x + t_ref[2 * asked_s[to, 2 * m + 1, 0] + 1]
            sendt[to, :, pl.ds(m * LANES, LANES)] = x

    @pl.loop(1, peers)
    def _(d):
        gather(peer(d))
        vec_copy(d).start()
        tile_copy(d).start()

    gather(me)
    own_vec = pltpu.make_async_copy(
        sendv.at[pl.ds(me * cap, cap)], gotv.at[pl.ds(me * cap, cap)], local_sem.at[0]
    )
    own_tile = pltpu.make_async_copy(sendt.at[me], gott.at[me], local_sem.at[1])
    own_vec.start()
    own_tile.start()

    metric = metric_ref[...]

    @pl.loop(0, pairs // 4)
    def _(g):
        v = v_ref[pl.ds(g * 4, 4)].reshape(4 * WIDE, domain)
        w = jnp.dot(v, metric, preferred_element_type=F32).astype(BF16)
        w_ref[pl.ds(g * 4, 4)] = w.reshape(4, WIDE, domain)

    lane = lax.broadcasted_iota(jnp.int32, (cap, LANES), 1)
    hote[...] = jnp.zeros_like(hote)
    hoto[...] = jnp.zeros_like(hoto)
    for j in range(peers):
        hit = jnp.where(asked_v[j] == lane, 1.0, 0.0)
        for k in range(cap):
            hot = hoto if k % 2 else hote
            hot[pl.ds(j * blocks + k // 2, 1), :] = hit[k : k + 1]
    en64[pl.ds(0, width), :] = en_ref[...]
    en64[pl.ds(width, WIDE - width), :] = jnp.zeros((WIDE - width, pairs), F32)

    @pl.loop(1, peers)
    def _(d):
        vec_copy(d).wait()
        tile_copy(d).wait()

    own_vec.wait()
    own_tile.wait()

    @pl.loop(0, peers)
    def _(j):
        for k in range(cap):
            x = gott[j, :, pl.ds((k // 2) * LANES, LANES)].astype(F32)
            swapped = pltpu.roll(x, WIDE, 1)
            here, there = (swapped, x) if k % 2 else (x, swapped)
            ot_ref[2 * (j * cap + k)] = halves(here)[0].astype(BF16)
            ot_ref[2 * (j * cap + k) + 1] = halves(there)[1].astype(BF16)

    own_z, ret_z = vlo, vhi
    side = 2 * WIDE
    diagonal = (lax.broadcasted_iota(jnp.int32, (side, side), 0) < WIDE) == (
        lax.broadcasted_iota(jnp.int32, (side, side), 1) < WIDE
    )

    @pl.loop(0, batches // group)
    def _(g):
        outs = []
        for k in range(group):
            i = g * group + k
            a1, a2 = self_s[i], self_s[i + batches]
            b1, b2 = slot_s[i], slot_s[i + batches]
            wa = jnp.concatenate([w_ref[a1], w_ref[a2]], axis=0)
            vb = jnp.concatenate([gotv[b1], gotv[b2]], axis=0)
            x = lax.dot_general(wa, vb, NT, preferred_element_type=F32)
            x = jnp.where(diagonal, x, 0.0)
            xt = x.T.astype(BF16)
            x = x.astype(BF16)
            tb = jnp.concatenate([ot_ref[2 * b1], ot_ref[2 * b2 + 1]], axis=0)
            ta = jnp.concatenate([t_ref[2 * a1], t_ref[2 * a2 + 1]], axis=0)
            left = jnp.dot(x, tb, preferred_element_type=F32).astype(BF16)
            proj = jnp.dot(xt, ta, preferred_element_type=F32).astype(BF16)
            to_own = jnp.dot(left, xt, preferred_element_type=F32)
            to_other = jnp.dot(proj, x, preferred_element_type=F32)
            outs.append((i, to_own[:WIDE] + to_own[WIDE:], to_other[:WIDE] + to_other[WIDE:]))
        for i, to_own, to_other in outs:
            own_z[pl.ds(i, WIDE, stride=batches), :] = to_own
            ret_z[pl.ds(i, WIDE, stride=batches), :] = to_other

    hs = lax.broadcasted_iota(jnp.int32, (slots, couplings), 0) == slot_ref[...]
    hs = jnp.where(hs, 1.0, 0.0)
    hs = jnp.concatenate([hs[:, :batches], hs[:, batches:]], axis=0).astype(BF16)
    for r in range(WIDE):
        z = ret_z[pl.ds(r * batches, batches), :].astype(BF16)
        y = jnp.dot(hs, z, preferred_element_type=F32)
        ret32[pl.ds(r * slots, slots), :] = halves(y[:slots])[0] + halves(y[slots:])[1]

    def pack(to):
        for m in range(blocks):
            x = ret32[pl.ds(to * cap + 2 * m, WIDE, stride=slots), :]
            x = halves(x + pltpu.roll(x, WIDE, 1))[0]
            if 2 * m + 1 < cap:
                y = ret32[pl.ds(to * cap + 2 * m + 1, WIDE, stride=slots), :]
                x = x + halves(y + pltpu.roll(y, WIDE, 1))[1]
            sendr[to, :, pl.ds(m * LANES, LANES)] = x.astype(BF16)

    @pl.loop(1, peers)
    def _(d):
        pack(peer(d))
        back_copy(d).start()

    pack(me)
    own_back = pltpu.make_async_copy(sendr.at[me], gotr.at[me], local_sem.at[0])
    own_back.start()

    ho = lax.broadcasted_iota(jnp.int32, (pairs, couplings), 0) == self_ref[...]
    ho = jnp.where(ho, 1.0, 0.0).astype(BF16)
    for r in range(width):
        z = own_z[pl.ds(r * batches, batches), :].T
        z = jnp.concatenate([z[:WIDE], z[WIDE:]], axis=1).astype(BF16)
        own32[pl.ds(r * WIDE, WIDE), :] = lax.dot_general(z, ho, NT, preferred_element_type=F32)

    @pl.loop(1, peers)
    def _(d):
        back_copy(d).wait()

    own_back.wait()

    @pl.loop(0, peers)
    def _(j):
        for m in range(blocks):
            back32[pl.ds((j * blocks + m) * WIDE, WIDE), :] = gotr[
                j, :, pl.ds(m * LANES, LANES)
            ].astype(F32)

    hot_even = hote[...].astype(BF16)
    hot_odd = hoto[...].astype(BF16)
    count = count_ref[...]
    inside = lax.broadcasted_iota(jnp.int32, (WIDE, pairs), 0) < count
    en = en64[...]
    out32 = tscr
    for r in range(width):
        x = back32[pl.ds(r, peers * blocks, stride=WIDE), :].T.astype(BF16)
        y = jnp.dot(x[:WIDE], hot_even, preferred_element_type=F32)
        y = y + jnp.dot(x[WIDE:], hot_odd, preferred_element_type=F32)
        y = y + own32[pl.ds(r * WIDE, WIDE), :]
        z = (en + en[r : r + 1]) * amp32[pl.ds(r * width, WIDE), :] - y
        out32[pl.ds(r * width, WIDE), :] = jnp.where(inside & (r < count), z, 0.0)
    out_ref[...] = out32[pl.ds(0, rows), :].astype(BF16)


def per_device(amplitudes, pno_coef, metric, energies, pno_count, cpl_self, cpl_slot, partner_list):
    peers = lax.axis_size("pair")
    pairs, tile_size = amplitudes.shape
    width = energies.shape[1]
    domain = pno_coef.shape[2]
    couplings = cpl_self.shape[0]
    slots = partner_list.shape[0]
    cap = slots // peers
    blocks = -(-cap // 2)
    requests = jnp.broadcast_to(
        lax.rem(partner_list, pairs).reshape(peers, cap, 1), (peers, cap, LANES)
    )
    out = pl.pallas_call(
        functools.partial(kernel, peers, cap, width, 4),
        out_shape=jax.ShapeDtypeStruct((tile_size, pairs), BF16),
        in_specs=[SMEM] * 3 + [VMEM] * 8,
        out_specs=VMEM,
        scratch_shapes=[
            pltpu.VMEM((peers, cap, LANES), jnp.int32),
            pltpu.SMEM((peers, cap, LANES), jnp.int32),
            pltpu.VMEM((tile_size + 16, pairs), F32),
            pltpu.VMEM((WIDE * pairs, LANES), F32),
            pltpu.VMEM((WIDE * pairs, LANES), F32),
            pltpu.VMEM((WIDE * pairs, LANES), F32),
            pltpu.VMEM((pairs, WIDE, domain), BF16),
            pltpu.VMEM((pairs, WIDE, domain), BF16),
            pltpu.VMEM((2 * pairs, WIDE, LANES), BF16),
            pltpu.VMEM((slots, WIDE, domain), BF16),
            pltpu.VMEM((peers, WIDE, blocks * LANES), BF16),
            pltpu.VMEM((slots, WIDE, domain), BF16),
            pltpu.VMEM((peers, WIDE, blocks * LANES), BF16),
            pltpu.VMEM((2 * slots, WIDE, LANES), BF16),
            pltpu.VMEM((peers, WIDE, blocks * LANES), BF16),
            pltpu.VMEM((peers, WIDE, blocks * LANES), BF16),
            pltpu.VMEM((WIDE * slots, LANES), F32),
            pltpu.VMEM((WIDE * WIDE, pairs), F32),
            pltpu.VMEM((WIDE * peers * blocks, LANES), F32),
            pltpu.VMEM((peers * blocks, LANES), F32),
            pltpu.VMEM((peers * blocks, LANES), F32),
            pltpu.VMEM((WIDE, pairs), F32),
            pltpu.SemaphoreType.DMA((2,)),
        ]
        + [pltpu.SemaphoreType.DMA((peers,))] * 8,
        compiler_params=pltpu.CompilerParams(
            vmem_limit_bytes=LIMIT, collective_id=0, has_side_effects=True
        ),
    )(
        pno_count, cpl_self, cpl_slot,
        pno_count.reshape(1, pairs), cpl_self.reshape(1, couplings), cpl_slot.reshape(1, couplings),
        requests, energies.T, metric, amplitudes.T, pno_coef.transpose(1, 0, 2),
    )
    return out.T


def solution(mesh):
    return jax.shard_map(
        per_device,
        mesh=mesh,
        in_specs=(
            P(("groups", "pair"), None),
            P(("groups", "pair"), None, None),
            P("groups", None),
            P(("groups", "pair"), None),
            P(("groups", "pair")),
            P(("groups", "pair")),
            P(("groups", "pair")),
            P(("groups", "pair")),
        ),
        out_specs=P(("groups", "pair"), None),
        check_vma=False,
    )
```

```python
import functools

import jax
import jax.numpy as jnp
from jax import lax
from jax.experimental import pallas as pl
from jax.experimental.pallas import tpu as pltpu
from jax.sharding import PartitionSpec as P

F32 = jnp.float32
BF16 = jnp.bfloat16
VMEM = pl.BlockSpec(memory_space=pltpu.VMEM)
SMEM = pl.BlockSpec(memory_space=pltpu.SMEM)
LIMIT = 60 * 1024 * 1024
WIDE = 64
SKEW = 8
LANES = 128
NT = (((1,), (1,)), ((), ()))


def halves(x):
    lane = lax.broadcasted_iota(jnp.int32, x.shape, 1)
    return jnp.where(lane < WIDE, x, 0.0), jnp.where(lane < WIDE, 0.0, x)


def kernel(
    peers, cap, width, group,
    count_s, self_s, slot_s, count_ref, self_ref, slot_ref, req_ref, en_ref, metric_ref, amp_ref, pno_ref,
    out_ref,
    asked_v, asked_s, amp32, vlo, vhi, tscr, v_ref, w_ref, t_ref, sendv, sendt, gotv, gott, ot_ref,
    sendr, gotr, ret32, own32, back32, hote, hoto, en64,
    local_sem, req_send, req_recv, vec_send, vec_recv, tile_send, tile_recv, back_send, back_recv,
):
    me = lax.axis_index("pair")
    pairs = count_ref.shape[1]
    domain = metric_ref.shape[0]
    couplings = self_ref.shape[1]
    slots = peers * cap
    batches = couplings // 2
    blocks = gott.shape[2] // LANES
    pitch = pairs + SKEW
    bpitch = batches + SKEW
    spitch = slots + SKEW
    wpitch = WIDE + SKEW

    def peer(d):
        return lax.rem(me + d, peers)

    def remote(src, dst, send, recv, d):
        return pltpu.make_async_remote_copy(
            src_ref=src, dst_ref=dst, send_sem=send.at[d], recv_sem=recv.at[d],
            device_id={"pair": peer(d)}, device_id_type=pl.DeviceIdType.MESH,
        )

    def req_copy(d):
        return remote(req_ref.at[peer(d)], asked_v.at[me], req_send, req_recv, d)

    def vec_copy(d):
        return remote(
            sendv.at[pl.ds(peer(d) * cap, cap)], gotv.at[pl.ds(me * cap, cap)], vec_send, vec_recv, d
        )

    def tile_copy(d):
        return remote(sendt.at[peer(d)], gott.at[me], tile_send, tile_recv, d)

    def back_copy(d):
        return remote(sendr.at[peer(d)], gotr.at[me], back_send, back_recv, d)

    barrier = pltpu.get_barrier_semaphore()

    @pl.loop(1, peers)
    def _(d):
        pl.semaphore_signal(
            barrier, inc=1, device_id={"pair": peer(d)}, device_id_type=pl.DeviceIdType.MESH
        )

    pl.semaphore_wait(barrier, peers - 1)

    @pl.loop(1, peers)
    def _(d):
        req_copy(d).start()

    own_req = pltpu.make_async_copy(req_ref.at[me], asked_v.at[me], local_sem.at[0])
    own_req.start()

    for r in range(width):
        x = pno_ref[r].astype(F32)
        vlo[pl.ds(r * pitch, pairs), :] = x[:, :LANES]
        vhi[pl.ds(r * pitch, pairs), :] = x[:, LANES:]
    for r in range(width, WIDE):
        vlo[pl.ds(r * pitch, pairs), :] = jnp.zeros((pairs, LANES), F32)
        vhi[pl.ds(r * pitch, pairs), :] = jnp.zeros((pairs, LANES), F32)
    row = lax.broadcasted_iota(jnp.int32, (WIDE, LANES), 0)

    @pl.loop(0, pairs // 4)
    def _(g):
        for k in range(4):
            p = g * 4 + k
            live = row < count_s[p]
            lo = jnp.where(live, vlo[pl.ds(p, WIDE, stride=pitch), :], 0.0)
            hi = jnp.where(live, vhi[pl.ds(p, WIDE, stride=pitch), :], 0.0)
            v_ref[p, :, pl.ds(0, LANES)] = lo.astype(BF16)
            v_ref[p, :, pl.ds(LANES, LANES)] = hi.astype(BF16)

    @pl.loop(1, peers)
    def _(d):
        req_copy(d).wait()

    own_req.wait()
    to_scalar = pltpu.make_async_copy(asked_v, asked_s, local_sem.at[1])
    to_scalar.start()
    to_scalar.wait()

    def take_vectors(to):
        for k in range(cap):
            sendv[to * cap + k] = v_ref[asked_s[to, k, 0]]

    def take_tiles(to):
        for m in range(blocks):
            x = t_ref[2 * asked_s[to, 2 * m, 0]]
            if 2 * m + 1 < cap:
                x = x + t_ref[2 * asked_s[to, 2 * m + 1, 0] + 1]
            sendt[to, :, pl.ds(m * LANES, LANES)] = x

    @pl.loop(1, peers)
    def _(d):
        d = 1 + lax.rem(d + peers // 2 - 2, peers - 1)
        take_vectors(peer(d))
        vec_copy(d).start()

    take_vectors(me)
    own_vec = pltpu.make_async_copy(
        sendv.at[pl.ds(me * cap, cap)], gotv.at[pl.ds(me * cap, cap)], local_sem.at[0]
    )
    own_vec.start()

    rows = amp_ref.shape[0]
    amp32[pl.ds(0, rows), :] = amp_ref[...].astype(F32)
    amp32[pl.ds(rows, amp32.shape[0] - rows), :] = jnp.zeros((amp32.shape[0] - rows, pairs), F32)
    for r in range(WIDE):
        if r < width:
            x = amp32[pl.ds(r * width, WIDE), :]
            x = jnp.concatenate([x, x], axis=0).T
        else:
            x = jnp.zeros((pairs, LANES), F32)
        tscr[pl.ds(r * pitch, pairs), :] = x

    @pl.loop(0, pairs // 4)
    def _(g):
        for k in range(4):
            p = g * 4 + k
            left, right = halves(tscr[pl.ds(p, WIDE, stride=pitch), :])
            t_ref[2 * p] = left.astype(BF16)
            t_ref[2 * p + 1] = right.astype(BF16)

    @pl.loop(1, peers)
    def _(d):
        d = 1 + lax.rem(d + peers // 2 - 2, peers - 1)
        take_tiles(peer(d))
        tile_copy(d).start()

    take_tiles(me)
    own_tile = pltpu.make_async_copy(sendt.at[me], gott.at[me], local_sem.at[1])
    own_tile.start()

    metric = metric_ref[...]

    @pl.loop(0, pairs // 4)
    def _(g):
        v = v_ref[pl.ds(g * 4, 4)].reshape(4 * WIDE, domain)
        w = jnp.dot(v, metric, preferred_element_type=F32).astype(BF16)
        w_ref[pl.ds(g * 4, 4)] = w.reshape(4, WIDE, domain)

    lane = lax.broadcasted_iota(jnp.int32, (cap, LANES), 1)
    hote[...] = jnp.zeros_like(hote)
    hoto[...] = jnp.zeros_like(hoto)
    for j in range(peers):
        hit = jnp.where(asked_v[j] == lane, 1.0, 0.0)
        for k in range(cap):
            hot = hoto if k % 2 else hote
            hot[pl.ds(j * blocks + k // 2, 1), :] = hit[k : k + 1]
    en64[pl.ds(0, width), :] = en_ref[...]
    en64[pl.ds(width, WIDE - width), :] = jnp.zeros((WIDE - width, pairs), F32)

    @pl.loop(1, peers)
    def _(d):
        vec_copy(d).wait()
        tile_copy(d).wait()

    own_vec.wait()
    own_tile.wait()

    @pl.loop(0, peers)
    def _(j):
        for k in range(cap):
            x = gott[j, :, pl.ds((k // 2) * LANES, LANES)].astype(F32)
            swapped = pltpu.roll(x, WIDE, 1)
            here, there = (swapped, x) if k % 2 else (x, swapped)
            ot_ref[2 * (j * cap + k)] = halves(here)[0].astype(BF16)
            ot_ref[2 * (j * cap + k) + 1] = halves(there)[1].astype(BF16)

    own_z, ret_z = vlo, vhi
    side = 2 * WIDE
    diagonal = (lax.broadcasted_iota(jnp.int32, (side, side), 0) < WIDE) == (
        lax.broadcasted_iota(jnp.int32, (side, side), 1) < WIDE
    )

    @pl.loop(0, batches // group)
    def _(g):
        outs = []
        for k in range(group):
            i = g * group + k
            a1, a2 = self_s[i], self_s[i + batches]
            b1, b2 = slot_s[i], slot_s[i + batches]
            wa = jnp.concatenate([w_ref[a1], w_ref[a2]], axis=0)
            vb = jnp.concatenate([gotv[b1], gotv[b2]], axis=0)
            x = lax.dot_general(wa, vb, NT, preferred_element_type=F32)
            x = jnp.where(diagonal, x, 0.0)
            x = x.astype(BF16)
            xt = x.T
            tb = jnp.concatenate([ot_ref[2 * b1], ot_ref[2 * b2 + 1]], axis=0)
            ta = jnp.concatenate([t_ref[2 * a1], t_ref[2 * a2 + 1]], axis=0)
            left = jnp.dot(x, tb, preferred_element_type=F32).astype(BF16)
            proj = jnp.dot(xt, ta, preferred_element_type=F32).astype(BF16)
            to_own = jnp.dot(left, xt, preferred_element_type=F32)
            to_other = jnp.dot(proj, x, preferred_element_type=F32)
            outs.append((i, to_own[:WIDE] + to_own[WIDE:], to_other[:WIDE] + to_other[WIDE:]))
        for i, to_own, to_other in outs:
            own_z[pl.ds(i, WIDE, stride=bpitch), :] = to_own
            ret_z[pl.ds(i, WIDE, stride=bpitch), :] = to_other

    hs = lax.broadcasted_iota(jnp.int32, (slots, couplings), 0) == slot_ref[...]
    hs = jnp.where(hs, 1.0, 0.0)
    hs = jnp.concatenate([hs[:, :batches], hs[:, batches:]], axis=0).astype(BF16)
    for r in range(WIDE):
        z = ret_z[pl.ds(r * bpitch, batches), :].astype(BF16)
        y = jnp.dot(hs, z, preferred_element_type=F32)
        ret32[pl.ds(r * spitch, slots), :] = halves(y[:slots])[0] + halves(y[slots:])[1]

    def pack(to):
        for m in range(blocks):
            x = ret32[pl.ds(to * cap + 2 * m, WIDE, stride=spitch), :]
            x = halves(x + pltpu.roll(x, WIDE, 1))[0]
            if 2 * m + 1 < cap:
                y = ret32[pl.ds(to * cap + 2 * m + 1, WIDE, stride=spitch), :]
                x = x + halves(y + pltpu.roll(y, WIDE, 1))[1]
            sendr[to, :, pl.ds(m * LANES, LANES)] = x.astype(BF16)

    @pl.loop(1, peers)
    def _(d):
        pack(peer(d))
        back_copy(d).start()

    pack(me)
    own_back = pltpu.make_async_copy(sendr.at[me], gotr.at[me], local_sem.at[0])
    own_back.start()

    ho = lax.broadcasted_iota(jnp.int32, (pairs, couplings), 0) == self_ref[...]
    ho = jnp.where(ho, 1.0, 0.0).astype(BF16)
    for r in range(width):
        z = own_z[pl.ds(r * bpitch, batches), :].T
        z = jnp.concatenate([z[:WIDE], z[WIDE:]], axis=1).astype(BF16)
        own32[pl.ds(r * WIDE, WIDE), :] = lax.dot_general(z, ho, NT, preferred_element_type=F32)

    @pl.loop(1, peers)
    def _(d):
        back_copy(d).wait()

    own_back.wait()

    @pl.loop(0, peers)
    def _(j):
        for m in range(blocks):
            back32[pl.ds((j * blocks + m) * wpitch, WIDE), :] = gotr[
                j, :, pl.ds(m * LANES, LANES)
            ].astype(F32)

    hot_even = hote[...].astype(BF16)
    hot_odd = hoto[...].astype(BF16)
    count = count_ref[...]
    inside = lax.broadcasted_iota(jnp.int32, (WIDE, pairs), 0) < count
    en = en64[...]
    out32 = tscr
    for r in range(width):
        x = back32[pl.ds(r, peers * blocks, stride=wpitch), :].T.astype(BF16)
        y = jnp.dot(x[:WIDE], hot_even, preferred_element_type=F32)
        y = y + jnp.dot(x[WIDE:], hot_odd, preferred_element_type=F32)
        y = y + own32[pl.ds(r * WIDE, WIDE), :]
        z = (en + en[r : r + 1]) * amp32[pl.ds(r * width, WIDE), :] - y
        out32[pl.ds(r * width, WIDE), :] = jnp.where(inside & (r < count), z, 0.0)
    out_ref[...] = out32[pl.ds(0, rows), :].astype(BF16)


def per_device(amplitudes, pno_coef, metric, energies, pno_count, cpl_self, cpl_slot, partner_list):
    peers = lax.axis_size("pair")
    pairs, tile_size = amplitudes.shape
    width = energies.shape[1]
    domain = pno_coef.shape[2]
    couplings = cpl_self.shape[0]
    slots = partner_list.shape[0]
    cap = slots // peers
    blocks = -(-cap // 2)
    requests = jnp.broadcast_to(
        lax.rem(partner_list, pairs).reshape(peers, cap, 1), (peers, cap, LANES)
    )
    out = pl.pallas_call(
        functools.partial(kernel, peers, cap, width, 16),
        out_shape=jax.ShapeDtypeStruct((tile_size, pairs), BF16),
        in_specs=[SMEM] * 3 + [VMEM] * 8,
        out_specs=VMEM,
        scratch_shapes=[
            pltpu.VMEM((peers, cap, LANES), jnp.int32),
            pltpu.SMEM((peers, cap, LANES), jnp.int32),
            pltpu.VMEM((tile_size + 16, pairs), F32),
            pltpu.VMEM((WIDE * (max(pairs, couplings // 2) + SKEW), LANES), F32),
            pltpu.VMEM((WIDE * (max(pairs, couplings // 2) + SKEW), LANES), F32),
            pltpu.VMEM((WIDE * (max(pairs, couplings // 2) + SKEW), LANES), F32),
            pltpu.VMEM((pairs, WIDE, domain), BF16),
            pltpu.VMEM((pairs, WIDE, domain), BF16),
            pltpu.VMEM((2 * pairs, WIDE, LANES), BF16),
            pltpu.VMEM((slots, WIDE, domain), BF16),
            pltpu.VMEM((peers, WIDE, blocks * LANES), BF16),
            pltpu.VMEM((slots, WIDE, domain), BF16),
            pltpu.VMEM((peers, WIDE, blocks * LANES), BF16),
            pltpu.VMEM((2 * slots, WIDE, LANES), BF16),
            pltpu.VMEM((peers, WIDE, blocks * LANES), BF16),
            pltpu.VMEM((peers, WIDE, blocks * LANES), BF16),
            pltpu.VMEM((WIDE * (slots + SKEW), LANES), F32),
            pltpu.VMEM((WIDE * WIDE, pairs), F32),
            pltpu.VMEM(((WIDE + SKEW) * peers * blocks, LANES), F32),
            pltpu.VMEM((peers * blocks, LANES), F32),
            pltpu.VMEM((peers * blocks, LANES), F32),
            pltpu.VMEM((WIDE, pairs), F32),
            pltpu.SemaphoreType.DMA((2,)),
        ]
        + [pltpu.SemaphoreType.DMA((peers,))] * 8,
        compiler_params=pltpu.CompilerParams(
            vmem_limit_bytes=LIMIT, collective_id=0, has_side_effects=True
        ),
    )(
        pno_count, cpl_self, cpl_slot,
        pno_count.reshape(1, pairs), cpl_self.reshape(1, couplings), cpl_slot.reshape(1, couplings),
        requests, energies.T, metric, amplitudes.T, pno_coef.transpose(1, 0, 2),
    )
    return out.T


def solution(mesh):
    return jax.shard_map(
        per_device,
        mesh=mesh,
        in_specs=(
            P(("groups", "pair"), None),
            P(("groups", "pair"), None, None),
            P("groups", None),
            P(("groups", "pair"), None),
            P(("groups", "pair")),
            P(("groups", "pair")),
            P(("groups", "pair")),
            P(("groups", "pair")),
        ),
        out_specs=P(("groups", "pair"), None),
        check_vma=False,
    )
```

```python
import functools

import jax
import jax.numpy as jnp
from jax import lax
from jax.experimental import pallas as pl
from jax.experimental.pallas import tpu as pltpu
from jax.sharding import PartitionSpec as P

F32 = jnp.float32
BF16 = jnp.bfloat16
VMEM = pl.BlockSpec(memory_space=pltpu.VMEM)
SMEM = pl.BlockSpec(memory_space=pltpu.SMEM)
LIMIT = 60 * 1024 * 1024
WIDE = 64
SKEW = 8
LANES = 128
NT = (((1,), (1,)), ((), ()))


def halves(x):
    lane = lax.broadcasted_iota(jnp.int32, x.shape, 1)
    return jnp.where(lane < WIDE, x, 0.0), jnp.where(lane < WIDE, 0.0, x)


def kernel(
    peers, cap, width, group,
    count_s, self_s, slot_s, count_ref, self_ref, slot_ref, req_ref, en_ref, metric_ref, amp_ref, pno_ref,
    out_ref,
    asked_v, asked_s, amp32, vlo, vhi, tscr, v_ref, w_ref, t_ref, sendv, sendt, gotv, gott, ot_ref,
    sendr, gotr, ret32, own32, back32, hote, hoto, en64, x_ref,
    local_sem, req_send, req_recv, vec_send, vec_recv, tile_send, tile_recv, back_send, back_recv,
):
    me = lax.axis_index("pair")
    pairs = count_ref.shape[1]
    domain = metric_ref.shape[0]
    couplings = self_ref.shape[1]
    slots = peers * cap
    batches = couplings // 2
    blocks = gott.shape[2] // LANES
    pitch = pairs + SKEW
    bpitch = batches + SKEW
    spitch = slots + SKEW
    wpitch = WIDE + SKEW

    def peer(d):
        return lax.rem(me + d, peers)

    def remote(src, dst, send, recv, d):
        return pltpu.make_async_remote_copy(
            src_ref=src, dst_ref=dst, send_sem=send.at[d], recv_sem=recv.at[d],
            device_id={"pair": peer(d)}, device_id_type=pl.DeviceIdType.MESH,
        )

    def req_copy(d):
        return remote(req_ref.at[peer(d)], asked_v.at[me], req_send, req_recv, d)

    def vec_copy(d):
        return remote(
            sendv.at[pl.ds(peer(d) * cap, cap)], gotv.at[pl.ds(me * cap, cap)], vec_send, vec_recv, d
        )

    def tile_copy(d):
        return remote(sendt.at[peer(d)], gott.at[me], tile_send, tile_recv, d)

    def back_copy(d):
        return remote(sendr.at[peer(d)], gotr.at[me], back_send, back_recv, d)

    barrier = pltpu.get_barrier_semaphore()

    @pl.loop(1, peers)
    def _(d):
        pl.semaphore_signal(
            barrier, inc=1, device_id={"pair": peer(d)}, device_id_type=pl.DeviceIdType.MESH
        )

    pl.semaphore_wait(barrier, peers - 1)

    @pl.loop(1, peers)
    def _(d):
        req_copy(d).start()

    own_req = pltpu.make_async_copy(req_ref.at[me], asked_v.at[me], local_sem.at[0])
    own_req.start()

    for r in range(width):
        x = pno_ref[r].astype(F32)
        vlo[pl.ds(r * pitch, pairs), :] = x[:, :LANES]
        vhi[pl.ds(r * pitch, pairs), :] = x[:, LANES:]
    for r in range(width, WIDE):
        vlo[pl.ds(r * pitch, pairs), :] = jnp.zeros((pairs, LANES), F32)
        vhi[pl.ds(r * pitch, pairs), :] = jnp.zeros((pairs, LANES), F32)
    row = lax.broadcasted_iota(jnp.int32, (WIDE, LANES), 0)

    @pl.loop(0, pairs // 4)
    def _(g):
        for k in range(4):
            p = g * 4 + k
            live = row < count_s[p]
            lo = jnp.where(live, vlo[pl.ds(p, WIDE, stride=pitch), :], 0.0)
            hi = jnp.where(live, vhi[pl.ds(p, WIDE, stride=pitch), :], 0.0)
            v_ref[p, :, pl.ds(0, LANES)] = lo.astype(BF16)
            v_ref[p, :, pl.ds(LANES, LANES)] = hi.astype(BF16)

    @pl.loop(1, peers)
    def _(d):
        req_copy(d).wait()

    own_req.wait()
    to_scalar = pltpu.make_async_copy(asked_v, asked_s, local_sem.at[1])
    to_scalar.start()
    to_scalar.wait()

    def take_vectors(to):
        for k in range(cap):
            sendv[to * cap + k] = v_ref[asked_s[to, k, 0]]

    def take_tiles(to):
        for m in range(blocks):
            x = t_ref[2 * asked_s[to, 2 * m, 0]]
            if 2 * m + 1 < cap:
                x = x + t_ref[2 * asked_s[to, 2 * m + 1, 0] + 1]
            sendt[to, :, pl.ds(m * LANES, LANES)] = x

    @pl.loop(1, peers)
    def _(d):
        d = 1 + lax.rem(d + peers // 2 - 2, peers - 1)
        take_vectors(peer(d))
        vec_copy(d).start()

    take_vectors(me)
    own_vec = pltpu.make_async_copy(
        sendv.at[pl.ds(me * cap, cap)], gotv.at[pl.ds(me * cap, cap)], local_sem.at[0]
    )
    own_vec.start()

    rows = amp_ref.shape[0]
    amp32[pl.ds(0, rows), :] = amp_ref[...].astype(F32)
    amp32[pl.ds(rows, amp32.shape[0] - rows), :] = jnp.zeros((amp32.shape[0] - rows, pairs), F32)
    for r in range(WIDE):
        if r < width:
            x = amp32[pl.ds(r * width, WIDE), :]
            x = jnp.concatenate([x, x], axis=0).T
        else:
            x = jnp.zeros((pairs, LANES), F32)
        tscr[pl.ds(r * pitch, pairs), :] = x

    @pl.loop(0, pairs // 4)
    def _(g):
        for k in range(4):
            p = g * 4 + k
            left, right = halves(tscr[pl.ds(p, WIDE, stride=pitch), :])
            t_ref[2 * p] = left.astype(BF16)
            t_ref[2 * p + 1] = right.astype(BF16)

    @pl.loop(1, peers)
    def _(d):
        d = 1 + lax.rem(d + peers // 2 - 2, peers - 1)
        take_tiles(peer(d))
        tile_copy(d).start()

    take_tiles(me)
    own_tile = pltpu.make_async_copy(sendt.at[me], gott.at[me], local_sem.at[1])
    own_tile.start()

    metric = metric_ref[...]

    @pl.loop(0, pairs // 4)
    def _(g):
        v = v_ref[pl.ds(g * 4, 4)].reshape(4 * WIDE, domain)
        w = jnp.dot(v, metric, preferred_element_type=F32).astype(BF16)
        w_ref[pl.ds(g * 4, 4)] = w.reshape(4, WIDE, domain)

    lane = lax.broadcasted_iota(jnp.int32, (cap, LANES), 1)
    hote[...] = jnp.zeros_like(hote)
    hoto[...] = jnp.zeros_like(hoto)
    for j in range(peers):
        hit = jnp.where(asked_v[j] == lane, 1.0, 0.0)
        for k in range(cap):
            hot = hoto if k % 2 else hote
            hot[pl.ds(j * blocks + k // 2, 1), :] = hit[k : k + 1]
    en64[pl.ds(0, width), :] = en_ref[...]
    en64[pl.ds(width, WIDE - width), :] = jnp.zeros((WIDE - width, pairs), F32)

    @pl.loop(1, peers)
    def _(d):
        vec_copy(d).wait()

    own_vec.wait()

    own_z, ret_z = vlo, vhi
    side = 2 * WIDE
    diagonal = (lax.broadcasted_iota(jnp.int32, (side, side), 0) < WIDE) == (
        lax.broadcasted_iota(jnp.int32, (side, side), 1) < WIDE
    )

    @pl.loop(0, batches // group)
    def _(g):
        outs = []
        for k in range(group):
            i = g * group + k
            a1, a2 = self_s[i], self_s[i + batches]
            b1, b2 = slot_s[i], slot_s[i + batches]
            wa = jnp.concatenate([w_ref[a1], w_ref[a2]], axis=0)
            vb = jnp.concatenate([gotv[b1], gotv[b2]], axis=0)
            x = lax.dot_general(wa, vb, NT, preferred_element_type=F32)
            x = jnp.where(diagonal, x, 0.0).astype(BF16)
            ta = jnp.concatenate([t_ref[2 * a1], t_ref[2 * a2 + 1]], axis=0)
            proj = jnp.dot(x.T, ta, preferred_element_type=F32).astype(BF16)
            to_other = jnp.dot(proj, x, preferred_element_type=F32)
            outs.append((i, x, to_other[:WIDE] + to_other[WIDE:]))
        for i, x, to_other in outs:
            x_ref[i] = x
            ret_z[pl.ds(i, WIDE, stride=bpitch), :] = to_other

    hs = lax.broadcasted_iota(jnp.int32, (slots, couplings), 0) == slot_ref[...]
    hs = jnp.where(hs, 1.0, 0.0)
    hs = jnp.concatenate([hs[:, :batches], hs[:, batches:]], axis=0).astype(BF16)
    for r in range(WIDE):
        z = ret_z[pl.ds(r * bpitch, batches), :].astype(BF16)
        y = jnp.dot(hs, z, preferred_element_type=F32)
        ret32[pl.ds(r * spitch, slots), :] = halves(y[:slots])[0] + halves(y[slots:])[1]

    def pack(to):
        for m in range(blocks):
            x = ret32[pl.ds(to * cap + 2 * m, WIDE, stride=spitch), :]
            x = halves(x + pltpu.roll(x, WIDE, 1))[0]
            if 2 * m + 1 < cap:
                y = ret32[pl.ds(to * cap + 2 * m + 1, WIDE, stride=spitch), :]
                x = x + halves(y + pltpu.roll(y, WIDE, 1))[1]
            sendr[to, :, pl.ds(m * LANES, LANES)] = x.astype(BF16)

    @pl.loop(1, peers)
    def _(d):
        pack(peer(d))
        back_copy(d).start()

    pack(me)
    own_back = pltpu.make_async_copy(sendr.at[me], gotr.at[me], local_sem.at[2])
    own_back.start()

    @pl.loop(1, peers)
    def _(d):
        tile_copy(d).wait()

    own_tile.wait()

    @pl.loop(0, peers)
    def _(j):
        for k in range(cap):
            x = gott[j, :, pl.ds((k // 2) * LANES, LANES)].astype(F32)
            swapped = pltpu.roll(x, WIDE, 1)
            here, there = (swapped, x) if k % 2 else (x, swapped)
            ot_ref[2 * (j * cap + k)] = halves(here)[0].astype(BF16)
            ot_ref[2 * (j * cap + k) + 1] = halves(there)[1].astype(BF16)

    @pl.loop(0, batches // group)
    def _(g):
        outs = []
        for k in range(group):
            i = g * group + k
            b1, b2 = slot_s[i], slot_s[i + batches]
            x = x_ref[i]
            tb = jnp.concatenate([ot_ref[2 * b1], ot_ref[2 * b2 + 1]], axis=0)
            left = jnp.dot(x, tb, preferred_element_type=F32).astype(BF16)
            to_own = lax.dot_general(left, x, NT, preferred_element_type=F32)
            outs.append((i, to_own[:WIDE] + to_own[WIDE:]))
        for i, to_own in outs:
            own_z[pl.ds(i, WIDE, stride=bpitch), :] = to_own

    ho = lax.broadcasted_iota(jnp.int32, (pairs, couplings), 0) == self_ref[...]
    ho = jnp.where(ho, 1.0, 0.0).astype(BF16)
    for r in range(width):
        z = own_z[pl.ds(r * bpitch, batches), :].T
        z = jnp.concatenate([z[:WIDE], z[WIDE:]], axis=1).astype(BF16)
        own32[pl.ds(r * WIDE, WIDE), :] = lax.dot_general(z, ho, NT, preferred_element_type=F32)

    @pl.loop(1, peers)
    def _(d):
        back_copy(d).wait()

    own_back.wait()

    @pl.loop(0, peers)
    def _(j):
        for m in range(blocks):
            back32[pl.ds((j * blocks + m) * wpitch, WIDE), :] = gotr[
                j, :, pl.ds(m * LANES, LANES)
            ].astype(F32)

    hot_even = hote[...].astype(BF16)
    hot_odd = hoto[...].astype(BF16)
    count = count_ref[...]
    inside = lax.broadcasted_iota(jnp.int32, (WIDE, pairs), 0) < count
    en = en64[...]
    out32 = tscr
    for r in range(width):
        x = back32[pl.ds(r, peers * blocks, stride=wpitch), :].T.astype(BF16)
        y = jnp.dot(x[:WIDE], hot_even, preferred_element_type=F32)
        y = y + jnp.dot(x[WIDE:], hot_odd, preferred_element_type=F32)
        y = y + own32[pl.ds(r * WIDE, WIDE), :]
        z = (en + en[r : r + 1]) * amp32[pl.ds(r * width, WIDE), :] - y
        out32[pl.ds(r * width, WIDE), :] = jnp.where(inside & (r < count), z, 0.0)
    out_ref[...] = out32[pl.ds(0, rows), :].astype(BF16)


def per_device(amplitudes, pno_coef, metric, energies, pno_count, cpl_self, cpl_slot, partner_list):
    peers = lax.axis_size("pair")
    pairs, tile_size = amplitudes.shape
    width = energies.shape[1]
    domain = pno_coef.shape[2]
    couplings = cpl_self.shape[0]
    slots = partner_list.shape[0]
    cap = slots // peers
    blocks = -(-cap // 2)
    requests = jnp.broadcast_to(
        lax.rem(partner_list, pairs).reshape(peers, cap, 1), (peers, cap, LANES)
    )
    out = pl.pallas_call(
        functools.partial(kernel, peers, cap, width, 16),
        out_shape=jax.ShapeDtypeStruct((tile_size, pairs), BF16),
        in_specs=[SMEM] * 3 + [VMEM] * 8,
        out_specs=VMEM,
        scratch_shapes=[
            pltpu.VMEM((peers, cap, LANES), jnp.int32),
            pltpu.SMEM((peers, cap, LANES), jnp.int32),
            pltpu.VMEM((tile_size + 16, pairs), F32),
            pltpu.VMEM((WIDE * (max(pairs, couplings // 2) + SKEW), LANES), F32),
            pltpu.VMEM((WIDE * (max(pairs, couplings // 2) + SKEW), LANES), F32),
            pltpu.VMEM((WIDE * (max(pairs, couplings // 2) + SKEW), LANES), F32),
            pltpu.VMEM((pairs, WIDE, domain), BF16),
            pltpu.VMEM((pairs, WIDE, domain), BF16),
            pltpu.VMEM((2 * pairs, WIDE, LANES), BF16),
            pltpu.VMEM((slots, WIDE, domain), BF16),
            pltpu.VMEM((peers, WIDE, blocks * LANES), BF16),
            pltpu.VMEM((slots, WIDE, domain), BF16),
            pltpu.VMEM((peers, WIDE, blocks * LANES), BF16),
            pltpu.VMEM((2 * slots, WIDE, LANES), BF16),
            pltpu.VMEM((peers, WIDE, blocks * LANES), BF16),
            pltpu.VMEM((peers, WIDE, blocks * LANES), BF16),
            pltpu.VMEM((WIDE * (slots + SKEW), LANES), F32),
            pltpu.VMEM((WIDE * WIDE, pairs), F32),
            pltpu.VMEM(((WIDE + SKEW) * peers * blocks, LANES), F32),
            pltpu.VMEM((peers * blocks, LANES), F32),
            pltpu.VMEM((peers * blocks, LANES), F32),
            pltpu.VMEM((WIDE, pairs), F32),
            pltpu.VMEM((couplings // 2, 2 * WIDE, 2 * WIDE), BF16),
            pltpu.SemaphoreType.DMA((3,)),
        ]
        + [pltpu.SemaphoreType.DMA((peers,))] * 8,
        compiler_params=pltpu.CompilerParams(
            vmem_limit_bytes=LIMIT, collective_id=0, has_side_effects=True
        ),
    )(
        pno_count, cpl_self, cpl_slot,
        pno_count.reshape(1, pairs), cpl_self.reshape(1, couplings), cpl_slot.reshape(1, couplings),
        requests, energies.T, metric, amplitudes.T, pno_coef.transpose(1, 0, 2),
    )
    return out.T


def solution(mesh):
    return jax.shard_map(
        per_device,
        mesh=mesh,
        in_specs=(
            P(("groups", "pair"), None),
            P(("groups", "pair"), None, None),
            P("groups", None),
            P(("groups", "pair"), None),
            P(("groups", "pair")),
            P(("groups", "pair")),
            P(("groups", "pair")),
            P(("groups", "pair")),
        ),
        out_specs=P(("groups", "pair"), None),
        check_vma=False,
    )
```
